256 devices in a mesh: spec: 32 (over y, x, z_hi), pix: 8 (over z_lo, core).
Axes of the slice: x: 4, y: 4, z: 8 (z_hi: 2, z_lo: 4; z = z_hi * 4 + z_lo), core: 2. Of those that a mesh axis runs over, the one named last changes fastest.
Arguments:
- spectra: float32 [2, 16, 4096, 2048], P(None, None, 'pix', 'spec'), may hold values from -6 to 6
- dispersion: float32 [2048], replicated, may hold values from -3.140625 to 3.140625
- window_start: int32 [32], replicated, may hold values from -4 to 248, as said below
- window_width: int32 [32], replicated, may hold values from 8 to 16, as said below
- pupil: float32 [2, 2048, 4096], P(None, None, 'pix'), may hold values from -0.0625 to 0.0625
Outputs:
- focused: float32 [32, 16, 2048], P('spec', None, 'pix')
The draws below stay inside these ranges and needn't reach their ends.
Inputs may be any that keep to these rules, and one draw needn't show every extreme that they name: window_start[d] lies between d * 8 - 4 and d * 8; the first owner's window starts at -4 and the last owner's at 248. window_start[d] + window_width[d] lies between (d + 1) * 8 and (d + 1) * 8 + 4.
All inputs are finite; a program needn't handle non-finite values.
Results may differ from the reference program's by a relative error of at most 0.000067.
Values sent between devices are 32-bit elements; how exact they have to be, the bound alone decides.
A program may use at most 128 MiB of HBM per device.

```python
import math
import jax
import jax.numpy as jnp
from jax import lax

K = 2048
G = 256
PIXELS = 4096
INPUTS = 16
FOCI = 2048
HALO = 4
GD = 8
DEPTHS = 32


def window_offsets(key):
    first_key, second_key = jax.random.split(key)
    lower = jax.random.randint(first_key, (DEPTHS,), 0, HALO + 1, dtype=jnp.int32)
    upper = jax.random.randint(second_key, (DEPTHS,), 0, HALO + 1, dtype=jnp.int32)
    lower = lower.at[0].set(0).at[DEPTHS - 1].set(HALO)
    upper = upper.at[0].set(HALO).at[DEPTHS - 1].set(0)
    return (lower, upper)


def draw_window_start(key, part):
    lower, upper = window_offsets(key)
    owners = jnp.arange(DEPTHS, dtype=jnp.int32)
    return owners * GD - HALO + lower


def draw_window_width(key, part):
    lower, upper = window_offsets(key)
    owners = jnp.arange(DEPTHS, dtype=jnp.int32)
    begin_gate = owners * GD - HALO + lower
    end_gate = (owners + 1) * GD + upper
    return end_gate - begin_gate


def with_spikes(values, key, source, target, blocks, factor):
    owner, partner = [(jnp.arange(values.shape[dim]) // (values.shape[dim] // blocks)).reshape([-1 if axis == dim else 1 for axis in range(values.ndim)]) for dim in (source, target)]
    chosen = jax.random.permutation(key, blocks)[partner]
    strong = (owner == chosen) | (owner == (partner + blocks // 2) % blocks)
    return jnp.where(strong, factor * values, values)


def levels(rng, dims, shards, low, top_value):
    loudness, own = 1.0, jax.random.fold_in(rng, 6)
    for position, blocks in shards:
        heights = jnp.exp(jax.random.uniform(jax.random.fold_in(own, position), (blocks,), jnp.float32, low / len(shards), top_value / len(shards)))
        loudness = loudness * jnp.repeat(heights, dims[position] // blocks).reshape([-1 if axis == position else 1 for axis in range(len(dims))])
    return loudness


def gaussian(key, extent, deviation, limit, shards=(), held_as=jnp.bfloat16):
    result = jax.random.normal(key, extent, jnp.float32) * deviation
    if len(shards) > 0:
        result = levels(key, extent, shards, -0.22, 0.18) * result
    return jnp.clip(result, min=-limit, max=limit).astype(held_as)


def noise_with(rng, shape, scale, reach, shards, heavy, held_as=jnp.bfloat16):
    array = scale * jax.random.normal(rng, shape, jnp.float32)
    if shards:
        array = array * levels(rng, shape, shards, -0.22, 0.18)
    return jnp.clip(with_spikes(array, jax.random.fold_in(rng, 3), *heavy), -reach, reach).astype(held_as)


def setup_inputs(seed: int = 0) -> dict:
    arg_keys = jax.random.split(jax.random.key(seed), 6)
    spectra = gaussian(arg_keys[0], (2, INPUTS, PIXELS, K), 1.0, 6.0, ((2, 8), (3, 32)), jnp.float32)
    dispersion = jnp.clip(jax.random.uniform(arg_keys[1], (K,), jnp.float32, -3.140625, 3.140625), -3.140625, 3.140625)
    window_start = draw_window_start(jax.random.fold_in(arg_keys[5], 71), 0)
    window_width = draw_window_width(jax.random.fold_in(arg_keys[5], 71), 0)
    pupil = noise_with(arg_keys[4], (2, FOCI, PIXELS), (4 * PIXELS) ** -0.5, 0.0625, ((2, 8),), (2, 1, 8, 2.0), jnp.float32)
    return dict(spectra=spectra, dispersion=dispersion, window_start=window_start, window_width=window_width, pupil=pupil)


def gate_table(gate_index, wave_index, wave_phase, wave_total):
    product = gate_index[:, None] * wave_index[None, :] % wave_total
    angles = 2.0 * math.pi / wave_total * product.astype(jnp.float32) + wave_phase[None, :]
    factor = 1.0 / math.sqrt(wave_total)
    cosine = jnp.cos(angles) * factor
    sine_part = jnp.sin(angles) * factor
    real_row = jnp.stack([cosine, sine_part], axis=1)
    imag_row = jnp.stack([-sine_part, cosine], axis=1)
    return jnp.stack([real_row, imag_row], axis=1)

def apply_table(dft_table, spectra_block):
    return lax.dot_general(dft_table, spectra_block, (((2, 3), (0, 3)), ((), ())), precision=lax.Precision.HIGHEST, preferred_element_type=jnp.float32)

def project_pupil(field_part, pupil_part):
    return jnp.einsum('gip,fp->gif', field_part, pupil_part, precision=lax.Precision.HIGHEST)

def reference(spectra, dispersion, window_start, window_width, pupil):
    dft_table = gate_table(jnp.arange(G, dtype=jnp.int32), jnp.arange(K, dtype=jnp.int32), dispersion, K)
    block_size = min(PIXELS, 512)
    block_count = PIXELS // block_size

    def one_block(block_id):
        spectra_block = lax.dynamic_slice_in_dim(spectra, block_id * block_size, block_size, 2)
        return apply_table(dft_table, spectra_block)
    blocks = lax.map(one_block, jnp.arange(block_count, dtype=jnp.int32))
    gate_field = jnp.moveaxis(blocks, 0, 3).reshape(G, 2, INPUTS, PIXELS)
    real_part = project_pupil(gate_field[:, 0], pupil[0]) - project_pupil(gate_field[:, 1], pupil[1])
    imag_part = project_pupil(gate_field[:, 0], pupil[1]) + project_pupil(gate_field[:, 1], pupil[0])
    intensity = real_part * real_part + imag_part * imag_part
    gate_index = jnp.arange(G, dtype=jnp.int32)
    inside = ((gate_index[None, :] >= window_start[:, None]) & (gate_index[None, :] < window_start[:, None] + window_width[:, None])).astype(jnp.float32)
    return jnp.einsum('dg,gif->dif', inside, intensity, precision=lax.Precision.HIGHEST)
```

```python
import math

import jax
import jax.numpy as jnp
from jax import lax
from jax.experimental import pallas as pl
from jax.experimental.pallas import tpu as pltpu
from jax.sharding import PartitionSpec as P

K = 2048
MESH = pl.DeviceIdType.MESH
F32 = jnp.float32
BF16 = jnp.bfloat16
ROUNDS = 4
STEP = 2.0 * math.pi / K
NT = (((1,), (1,)), ((), ()))


def split(values):
    high = values.astype(BF16)
    return high, (values - high.astype(F32)).astype(BF16)


def kernel(
    spectra, disp, start, width, pupil, out,
    xbuf, xhl, th, tl, cosa, sina, cosb, sinb, pstage, ph, plo,
    part, zrecv, gsend, grecv, abuf, csend, own, crecv, frecv, hsend, hrecv,
    xs, xr, zs, zr, gs, gr, cs, cr, fs, fr, hs, hr, ps,
):
    s = lax.axis_index("spec")
    p = lax.axis_index("pix")
    me = s // 2
    zh = s % 2
    y = me // 4
    x = me % 4
    zl = p // 2
    co = p % 2
    partner = {"spec": s + 1 - 2 * zh}
    sibling = {"pix": zl * 2 + 1 - co}
    before = {"spec": (s + 31) % 32}
    after = {"spec": (s + 1) % 32}

    def peer(t):
        return ((y + t // 4) % 4) * 4 + (x + t % 4) % 4

    def along(dz):
        return (zl + dz) % 4

    barrier = pltpu.get_barrier_semaphore()

    def greet(t, carry):
        pl.semaphore_signal(
            barrier, inc=1, device_id={"spec": peer(t) * 2 + zh}, device_id_type=MESH
        )
        return carry

    lax.fori_loop(1, 16, greet, 0)
    for device in (partner, sibling, before, after):
        pl.semaphore_signal(barrier, inc=1, device_id=device, device_id_type=MESH)
    for dz in (1, 2, 3):
        pl.semaphore_signal(
            barrier, inc=1, device_id={"pix": along(dz) * 2 + co}, device_id_type=MESH
        )
    pl.semaphore_wait(barrier, 22)

    def block(r, j):
        return spectra.at[
            :, r * 4 + j // 4, :, pl.ds(pl.multiple_of((j % 4) * 128, 128), 128)
        ]

    def send_round(r, carry):
        def send(t, inner):
            j = peer(t)
            pltpu.make_async_remote_copy(
                src_ref=block(r, j), dst_ref=xbuf.at[r, me], send_sem=xs.at[0],
                recv_sem=xr.at[r], device_id={"spec": j * 2 + zh}, device_id_type=MESH,
            ).start()
            return inner

        lax.fori_loop(1, 16, send, 0)
        pltpu.make_async_copy(block(r, me), xbuf.at[r, me], xr.at[r]).start()
        return carry

    lax.fori_loop(0, ROUNDS, send_round, 0)

    def fetch(n, slot):
        return pltpu.make_async_copy(
            pupil.at[n // 4, pl.ds((n % 4) * 512, 512)], pstage.at[slot], ps.at[slot]
        )

    fetch(0, 0).start()

    lane = lax.broadcasted_iota(jnp.int32, (8, K), 1)
    cin = (lane // 64) % 2
    wave = (lane // 128) * 128 + zh * 64 + lane % 64
    phase = jnp.broadcast_to(disp[...], (8, K))
    up = pltpu.roll(phase, 64, 1)
    down = pltpu.roll(phase, K - 64, 1)
    phase = jnp.where(cin == zh, phase, jnp.where(cin == 1, up, down))
    fine = lax.broadcasted_iota(jnp.int32, (8, K), 0)
    beta = STEP * ((fine * wave - cin * 512) & (K - 1)).astype(F32) + phase
    scale = 1.0 / math.sqrt(K)
    cosb[...] = jnp.cos(beta) * scale
    sinb[...] = jnp.sin(beta) * scale

    def coarse(n, carry):
        row = lax.broadcasted_iota(jnp.int32, (8, K), 0) + n * 8
        zg = jnp.where(row < 16, 1 - zh, zh)
        q = (row % 16) * 2 + zg
        alpha = STEP * ((8 * q * wave) & (K - 1)).astype(F32)
        cosa[pl.ds(pl.multiple_of(n * 8, 8), 8), :] = jnp.cos(alpha)
        sina[pl.ds(pl.multiple_of(n * 8, 8), 8), :] = jnp.sin(alpha)
        return carry

    lax.fori_loop(0, 4, coarse, 0)

    def rows(n, carry):
        ca = cosa[pl.ds(n, 1), :]
        sa = sina[pl.ds(n, 1), :]
        real = ca * cosb[...] - sa * sinb[...]
        imag = -(sa * cosb[...] + ca * sinb[...])
        high, low = split(jnp.concatenate([real, imag], axis=0))
        at = pl.ds(pl.multiple_of(n * 16, 16), 16)
        th[at, :] = high
        tl[at, :] = low
        return carry

    lax.fori_loop(0, 32, rows, 0)

    def convert(n, carry):
        slot = n % 2

        @pl.when(n < 7)
        def _():
            fetch(n + 1, 1 - slot).start()

        fetch(n, slot).wait()

        def piece(m, inner):
            high, low = split(pstage[slot, pl.ds(pl.multiple_of(m * 64, 64), 64), :])
            at = pl.ds(pl.multiple_of((n % 4) * 512 + m * 64, 64), 64)
            ph[n // 4, at, :] = high
            plo[n // 4, at, :] = low
            return inner

        lax.fori_loop(0, 8, piece, 0)
        return carry

    lax.fori_loop(0, 8, convert, 0)

    def await_all(ref, sem):
        pltpu.make_async_copy(ref, ref, sem).wait()

    def half_copy(r):
        return pltpu.make_async_remote_copy(
            src_ref=part.at[r, 0], dst_ref=zrecv.at[r], send_sem=zs.at[r],
            recv_sem=zr.at[r], device_id=partner, device_id_type=MESH,
        )

    def core_copy(r):
        return pltpu.make_async_remote_copy(
            src_ref=csend.at[r], dst_ref=crecv.at[r], send_sem=cs.at[r],
            recv_sem=cr.at[r], device_id=sibling, device_id_type=MESH,
        )

    def transform(r):
        await_all(xbuf.at[r], xr.at[r])

        def piece(n, carry):
            high, low = split(xbuf[r, n].reshape(128, 128))
            at = pl.ds(pl.multiple_of(n * 128, 128), 128)
            xhl[at, 0:128] = high
            xhl[at, 128:256] = low
            return carry

        lax.fori_loop(0, 16, piece, 0)
        for half in (0, 1):
            at = slice(half * 256, half * 256 + 256)
            both = jnp.dot(th[at, :], xhl[...], preferred_element_type=F32)
            rest = jnp.dot(tl[at, :], xhl[:, 0:128], preferred_element_type=F32)
            part[r, half] = both[:, 0:128] + (both[:, 128:256] + rest)
            if half == 0:
                half_copy(r).start()

    def hand_out(r):
        half_copy(r).wait_recv()
        gsend[r] = (part[r, 1] + zrecv[r]).reshape(16, 16, 128)

        def send(t, carry):
            j = peer(t)
            pltpu.make_async_remote_copy(
                src_ref=gsend.at[r, j], dst_ref=grecv.at[r, me], send_sem=gs.at[0],
                recv_sem=gr.at[r], device_id={"spec": j * 2 + zh}, device_id_type=MESH,
            ).start()
            return carry

        lax.fori_loop(1, 16, send, 0)
        pltpu.make_async_copy(gsend.at[r, me], grecv.at[r, me], gr.at[r]).start()

    def project(r):
        await_all(grecv.at[r], gr.at[r])
        for i in range(4):
            real = jnp.concatenate([grecv[r, i * 4 + b, 0:8, :] for b in range(4)], axis=1)
            imag = jnp.concatenate([grecv[r, i * 4 + b, 8:16, :] for b in range(4)], axis=1)
            abuf[i * 8 : i * 8 + 8, 0:512] = real
            abuf[i * 8 : i * 8 + 8, 512:1024] = -imag
            abuf[32 + i * 8 : 40 + i * 8, 0:512] = imag
            abuf[32 + i * 8 : 40 + i * 8, 512:1024] = real
        high, low = split(abuf[...])
        stack = jnp.concatenate([high, low], axis=0)

        def product(b, core):
            at = pl.ds(pl.multiple_of((b * 2 + core) * 256, 256), 256)
            both = lax.dot_general(
                stack[:, 0:512], ph[0, at, :], NT, preferred_element_type=F32
            ) + lax.dot_general(stack[:, 512:1024], ph[1, at, :], NT, preferred_element_type=F32)
            rest = lax.dot_general(
                high[:, 0:512], plo[0, at, :], NT, preferred_element_type=F32
            ) + lax.dot_general(high[:, 512:1024], plo[1, at, :], NT, preferred_element_type=F32)
            return both[0:64] + (both[64:128] + rest)

        for b in range(4):
            csend[r, b] = product(b, 1 - co)
        core_copy(r).start()
        for b in range(4):
            own[r, b] = product(b, co)

    def along_copy(r, dz):
        return pltpu.make_async_remote_copy(
            src_ref=own.at[r, along(dz)], dst_ref=frecv.at[r, dz - 1], send_sem=fs.at[r, dz - 1],
            recv_sem=fr.at[r, dz - 1], device_id={"pix": along(dz) * 2 + co}, device_id_type=MESH,
        )

    def combine(r):
        core_copy(r).wait_recv()
        own[r] = own[r] + crecv[r]
        for dz in (1, 2, 3):
            along_copy(r, dz).start()

    gate = s * 8 + lax.broadcasted_iota(jnp.int32, (8, 256), 0)

    def weight(owner):
        first = start[owner]
        return ((gate >= first) & (gate < first + width[owner])).astype(F32)

    def finish(r):
        for dz in (1, 2, 3):
            along_copy(r, dz).wait_recv()
        total = own[r, zl] + (frecv[r, 0] + (frecv[r, 1] + frecv[r, 2]))
        power = total[0:32] * total[0:32] + total[32:64] * total[32:64]
        for n, owner in enumerate((s, (s + 31) % 32, (s + 1) % 32)):
            w = weight(owner)
            for i in range(4):
                hsend[n, r, i : i + 1, :] = jnp.sum(
                    power[i * 8 : i * 8 + 8] * w, axis=0, keepdims=True
                )

    def turn(n, carry):
        pl.when(n < 4)(lambda: transform(n))

        @pl.when((n >= 1) & (n < 4))
        def _():
            project(n - 1)
            combine(n - 1)

        pl.when((n >= 2) & (n < 5))(lambda: finish(n - 2))
        pl.when(n < 4)(lambda: hand_out(n))

        @pl.when(n == 4)
        def _():
            project(n - 1)
            combine(n - 1)
            finish(n - 1)

        return carry

    lax.fori_loop(0, 5, turn, 0)

    copies = []
    for n, device in ((1, before), (2, after)):
        copy = pltpu.make_async_remote_copy(
            src_ref=hsend.at[n], dst_ref=hrecv.at[n - 1], send_sem=hs.at[n - 1],
            recv_sem=hr.at[n - 1], device_id=device, device_id_type=MESH,
        )
        copy.start()
        copies.append(copy)

    def sent(r, carry):
        await_all(xbuf.at[r, pl.ds(0, 15)], xs.at[0])
        await_all(gsend.at[r, pl.ds(0, 15)], gs.at[0])
        half_copy(r).wait_send()
        core_copy(r).wait_send()
        for dz in (1, 2, 3):
            along_copy(r, dz).wait_send()
        return carry

    lax.fori_loop(0, ROUNDS, sent, 0)
    for copy in copies:
        copy.wait()
    for r in range(ROUNDS):
        out[r * 4 : r * 4 + 4, :] = hsend[0, r] + (hrecv[0, r] + hrecv[1, r])


def local(spectra, dispersion, window_start, window_width, pupil):
    vmem = pltpu.VMEM
    dma = pltpu.SemaphoreType.DMA
    hbm = pl.BlockSpec(memory_space=pl.ANY)
    smem = pl.BlockSpec(memory_space=pltpu.SMEM)
    focused = pl.pallas_call(
        kernel,
        out_shape=jax.ShapeDtypeStruct((16, 256), F32),
        in_specs=[hbm, pl.BlockSpec(memory_space=pltpu.VMEM), smem, smem, hbm],
        out_specs=pl.BlockSpec(memory_space=pltpu.VMEM),
        scratch_shapes=[
            vmem((4, 16, 2, 64, 128), F32),
            vmem((K, 256), BF16),
            vmem((512, K), BF16),
            vmem((512, K), BF16),
            vmem((32, K), F32),
            vmem((32, K), F32),
            vmem((8, K), F32),
            vmem((8, K), F32),
            vmem((2, 512, 512), F32),
            vmem((2, 2048, 512), BF16),
            vmem((2, 2048, 512), BF16),
            vmem((4, 2, 256, 128), F32),
            vmem((4, 256, 128), F32),
            vmem((4, 16, 16, 128), F32),
            vmem((4, 16, 16, 128), F32),
            vmem((64, 1024), F32),
            vmem((4, 4, 64, 256), F32),
            vmem((4, 4, 64, 256), F32),
            vmem((4, 4, 64, 256), F32),
            vmem((4, 3, 64, 256), F32),
            vmem((3, 4, 4, 256), F32),
            vmem((2, 4, 4, 256), F32),
            dma((1,)), dma((4,)), dma((4,)), dma((4,)), dma((1,)), dma((4,)),
            dma((4,)), dma((4,)), dma((4, 3)), dma((4, 3)), dma((2,)), dma((2,)), dma((2,)),
        ],
        compiler_params=pltpu.CompilerParams(
            collective_id=0, has_side_effects=True, vmem_limit_bytes=56 * 2**20
        ),
    )(
        jnp.swapaxes(spectra, 2, 3),
        dispersion.reshape(1, K),
        window_start,
        window_width,
        pupil,
    )
    return focused[None]


def solution(mesh):
    in_specs = (P(None, None, "pix", "spec"), P(), P(), P(), P(None, None, "pix"))
    out_specs = P("spec", None, "pix")
    return jax.shard_map(local, mesh=mesh, in_specs=in_specs, out_specs=out_specs, check_vma=False)
```

```python
import math

import jax
import jax.numpy as jnp
from jax import lax
from jax.experimental import pallas as pl
from jax.experimental.pallas import tpu as pltpu
from jax.sharding import PartitionSpec as P

K = 2048
MESH = pl.DeviceIdType.MESH
F32 = jnp.float32
BF16 = jnp.bfloat16
ROUNDS = 8
STEP = 2.0 * math.pi / K
NT = (((1,), (1,)), ((), ()))


def split(values):
    high = values.astype(BF16)
    return high, (values - high.astype(F32)).astype(BF16)


def kernel(
    spectra, disp, start, width, pupil, out,
    staged, packed, xbuf, xhl, th, tl, cosa, sina, cosb, sinb, pstage, ph, plo,
    part, zrecv, gsend, grecv, abuf, csend, own, crecv, frecv, hsend, hrecv,
    ls, xs, xr, zs, zr, gs, gr, cs, cr, fs, fr, hs, hr, ps,
):
    s = lax.axis_index("spec")
    p = lax.axis_index("pix")
    me = s // 2
    zh = s % 2
    y = me // 4
    x = me % 4
    zl = p // 2
    co = p % 2
    partner = {"spec": s + 1 - 2 * zh}
    sibling = {"pix": zl * 2 + 1 - co}
    before = {"spec": (s + 31) % 32}
    after = {"spec": (s + 1) % 32}

    def peer(t):
        return ((y + t // 4) % 4) * 4 + (x + t % 4) % 4

    def along(dz):
        return (zl + dz) % 4

    barrier = pltpu.get_barrier_semaphore()

    def greet(t, carry):
        pl.semaphore_signal(
            barrier, inc=1, device_id={"spec": peer(t) * 2 + zh}, device_id_type=MESH
        )
        return carry

    lax.fori_loop(1, 16, greet, 0)
    for device in (partner, sibling, before, after):
        pl.semaphore_signal(barrier, inc=1, device_id=device, device_id_type=MESH)
    for dz in (1, 2, 3):
        pl.semaphore_signal(
            barrier, inc=1, device_id={"pix": along(dz) * 2 + co}, device_id_type=MESH
        )
    left = lax.broadcasted_iota(jnp.int32, (64, 128), 1) < 64
    left8 = lax.broadcasted_iota(jnp.int32, (8, 128), 1) < 64

    def load(r):
        return pltpu.make_async_copy(spectra.at[:, pl.ds(r * 2, 2)], staged.at[r], ls.at[r])

    def pack(r):
        load(r).wait()
        for i in range(2):
            for m in range(4):
                at = slice(m * 128, m * 128 + 128)
                real = staged[r, 0, i, :, at]
                imag = staged[r, 1, i, :, at]
                packed[r, i * 8 + m * 2] = jnp.where(left, real, pltpu.roll(imag, 64, 1))
                packed[r, i * 8 + m * 2 + 1] = jnp.where(left, pltpu.roll(real, 64, 1), imag)

    def send_blocks(r):
        def send(t, carry):
            j = peer(t)
            pltpu.make_async_remote_copy(
                src_ref=packed.at[r, j], dst_ref=xbuf.at[r, me], send_sem=xs.at[0],
                recv_sem=xr.at[r], device_id={"spec": j * 2 + zh}, device_id_type=MESH,
            ).start()
            return carry

        lax.fori_loop(1, 16, send, 0)
        pltpu.make_async_copy(packed.at[r, me], xbuf.at[r, me], xr.at[r]).start()

    for r in range(ROUNDS):
        load(r).start()
    pack(0)
    pl.semaphore_wait(barrier, 22)
    send_blocks(0)
    pack(1)
    send_blocks(1)

    def fetch(n, slot):
        return pltpu.make_async_copy(
            pupil.at[n // 4, pl.ds((n % 4) * 512, 512)], pstage.at[slot], ps.at[slot]
        )

    fetch(0, 0).start()

    HALF = K // 2
    lane = lax.broadcasted_iota(jnp.int32, (8, HALF), 1)
    wave = (lane // 64) * 128 + zh * 64 + lane % 64
    pieces = []
    for m in range(8):
        a = jnp.broadcast_to(disp[:, m * 256 : m * 256 + 128], (8, 128))
        b = jnp.broadcast_to(disp[:, m * 256 + 128 : m * 256 + 256], (8, 128))
        lower = jnp.where(left8, a, pltpu.roll(b, 64, 1))
        upper = jnp.where(left8, pltpu.roll(a, 64, 1), b)
        pieces.append(jnp.where(zh == 0, lower, upper))
    phase = jnp.concatenate(pieces, axis=1)
    fine = lax.broadcasted_iota(jnp.int32, (8, HALF), 0)
    beta = STEP * ((fine * wave) & (K - 1)).astype(F32) + phase
    scale = 1.0 / math.sqrt(K)
    cosb[...] = jnp.cos(beta) * scale
    sinb[...] = jnp.sin(beta) * scale

    def coarse(n, carry):
        row = lax.broadcasted_iota(jnp.int32, (8, HALF), 0) + n * 8
        zg = jnp.where(row < 16, 1 - zh, zh)
        q = (row % 16) * 2 + zg
        alpha = STEP * ((8 * q * wave) & (K - 1)).astype(F32)
        cosa[pl.ds(pl.multiple_of(n * 8, 8), 8), :] = jnp.cos(alpha)
        sina[pl.ds(pl.multiple_of(n * 8, 8), 8), :] = jnp.sin(alpha)
        return carry

    lax.fori_loop(0, 4, coarse, 0)

    def rows(n, carry):
        ca = cosa[pl.ds(n, 1), :]
        sa = sina[pl.ds(n, 1), :]
        real = ca * cosb[...] - sa * sinb[...]
        imag = -(sa * cosb[...] + ca * sinb[...])
        high, low = split(jnp.concatenate([real, imag], axis=0))
        at = pl.ds(pl.multiple_of(n * 16, 16), 16)
        th[at, :] = high
        tl[at, :] = low
        return carry

    lax.fori_loop(0, 32, rows, 0)

    def convert(n, carry):
        slot = n % 2

        @pl.when(n < 7)
        def _():
            fetch(n + 1, 1 - slot).start()

        fetch(n, slot).wait()

        def piece(m, inner):
            high, low = split(pstage[slot, pl.ds(pl.multiple_of(m * 64, 64), 64), :])
            at = pl.ds(pl.multiple_of((n % 4) * 512 + m * 64, 64), 64)
            ph[n // 4, at, :] = high
            plo[n // 4, at, :] = low
            return inner

        lax.fori_loop(0, 8, piece, 0)
        return carry

    def convert_some(first, last):
        lax.fori_loop(first, last, convert, 0)

    convert_some(0, 4)

    def await_all(ref, sem):
        pltpu.make_async_copy(ref, ref, sem).wait()

    def half_copy(r, k):
        return pltpu.make_async_remote_copy(
            src_ref=part.at[r, k], dst_ref=zrecv.at[r, k], send_sem=zs.at[r, k],
            recv_sem=zr.at[r, k], device_id=partner, device_id_type=MESH,
        )

    def core_copy(r, k):
        return pltpu.make_async_remote_copy(
            src_ref=csend.at[r, k], dst_ref=crecv.at[r, k], send_sem=cs.at[r, k],
            recv_sem=cr.at[r, k], device_id=sibling, device_id_type=MESH,
        )

    def along_copy(r, k):
        return pltpu.make_async_remote_copy(
            src_ref=own.at[r, k], dst_ref=frecv.at[r, k], send_sem=fs.at[r, k],
            recv_sem=fr.at[r, k], device_id={"pix": along(k + 1) * 2 + co}, device_id_type=MESH,
        )

    def transform(r):
        await_all(xbuf.at[r], xr.at[r])

        def piece(n, carry):
            high, low = split(xbuf[r, pl.ds(n * 2, 2)].reshape(128, 128))
            at = pl.ds(pl.multiple_of(n * 128, 128), 128)
            xhl[at, 0:128] = high
            xhl[at, 128:256] = low
            return carry

        lax.fori_loop(0, 8, piece, 0)
        for half in (0, 1):
            at = slice(half * 256, half * 256 + 256)
            both = jnp.dot(th[at, :], xhl[...], preferred_element_type=F32)
            rest = jnp.dot(tl[at, :], xhl[:, 0:128], preferred_element_type=F32)
            done = (both[:, 0:128] + (both[:, 128:256] + rest)).reshape(16, 2, 8, 128)
            straight = done[:, 0].reshape(128, 128)
            crossed = pltpu.roll(done[:, 1].reshape(128, 128), 64, 1)
            left128 = lax.broadcasted_iota(jnp.int32, (128, 128), 1) < 64
            field = straight + jnp.where(left128, -crossed, crossed)
            part[r, half * 2] = field[0:64]
            part[r, half * 2 + 1] = field[64:128]
            if half == 0:
                half_copy(r, 0).start()
                half_copy(r, 1).start()

    def hand_out(r):
        def send(j):
            @pl.when(j != me)
            def _():
                pltpu.make_async_remote_copy(
                    src_ref=gsend.at[r, j], dst_ref=grecv.at[r, me], send_sem=gs.at[0],
                    recv_sem=gr.at[r], device_id={"spec": j * 2 + zh}, device_id_type=MESH,
                ).start()

        def ordered(t, carry):
            send(carry + ((t + me) % 8))
            return carry

        for k in (0, 1):
            half_copy(r, k).wait_recv()
            gsend[r, pl.ds(k * 8, 8)] = (part[r, 2 + k] + zrecv[r, k]).reshape(8, 8, 128)
            lax.fori_loop(0, 8, ordered, k * 8)
        pltpu.make_async_copy(gsend.at[r, me], grecv.at[r, me], gr.at[r]).start()

    def project(r):
        await_all(grecv.at[r], gr.at[r])
        for i in range(2):
            for m in range(4):
                a = grecv[r, i * 8 + m * 2]
                b = grecv[r, i * 8 + m * 2 + 1]
                real = jnp.where(left8, a, pltpu.roll(b, 64, 1))
                imag = jnp.where(left8, pltpu.roll(a, 64, 1), b)
                row = i * 8
                col = m * 128
                abuf[row : row + 8, col : col + 128] = real
                abuf[row : row + 8, 512 + col : 640 + col] = -imag
                abuf[16 + row : 24 + row, col : col + 128] = imag
                abuf[16 + row : 24 + row, 512 + col : 640 + col] = real
        high, low = split(abuf[...])
        stack = jnp.concatenate([high, low], axis=0)

        def product(b, core):
            at = pl.ds(pl.multiple_of((b * 2 + core) * 256, 256), 256)
            both = lax.dot_general(
                stack[:, 0:512], ph[0, at, :], NT, preferred_element_type=F32
            ) + lax.dot_general(stack[:, 512:1024], ph[1, at, :], NT, preferred_element_type=F32)
            rest = lax.dot_general(
                high[:, 0:512], plo[0, at, :], NT, preferred_element_type=F32
            ) + lax.dot_general(high[:, 512:1024], plo[1, at, :], NT, preferred_element_type=F32)
            return both[0:32] + (both[32:64] + rest)

        def give(k, carry):
            csend[r, k] = product(along(k + 1), 1 - co)
            core_copy(r, k).start()
            return carry

        lax.fori_loop(0, 4, give, 0)

        def pass_on(k, carry):
            mine = product(along(k + 1), co)
            core_copy(r, k).wait_recv()
            own[r, k] = mine + crecv[r, k]

            @pl.when(k < 3)
            def _():
                along_copy(r, k).start()

            return carry

        lax.fori_loop(0, 4, pass_on, 0)

    gate = s * 8 + lax.broadcasted_iota(jnp.int32, (8, 256), 0)

    def weight(owner):
        first = start[owner]
        return ((gate >= first) & (gate < first + width[owner])).astype(F32)

    def finish(r):
        for k in range(3):
            along_copy(r, k).wait_recv()
        total = own[r, 3] + (frecv[r, 0] + (frecv[r, 1] + frecv[r, 2]))
        power = total[0:16] * total[0:16] + total[16:32] * total[16:32]
        for n, owner in enumerate((s, (s + 31) % 32, (s + 1) % 32)):
            w = weight(owner)
            for i in range(2):
                hsend[n, r, i : i + 1, :] = jnp.sum(
                    power[i * 8 : i * 8 + 8] * w, axis=0, keepdims=True
                )

    def turn(n, carry):
        pl.when(n < 8)(lambda: transform(n))
        pl.when(n < 6)(lambda: pack(n + 2))
        pl.when((n >= 1) & (n < 9))(lambda: hand_out(n - 1))
        pl.when(n < 6)(lambda: send_blocks(n + 2))
        pl.when(n == 0)(lambda: convert_some(4, 8))
        pl.when((n >= 2) & (n < 10))(lambda: project(n - 2))
        pl.when(n >= 3)(lambda: finish(n - 3))
        return carry

    lax.fori_loop(0, ROUNDS + 3, turn, 0)

    copies = []
    for n, device in ((1, before), (2, after)):
        copy = pltpu.make_async_remote_copy(
            src_ref=hsend.at[n], dst_ref=hrecv.at[n - 1], send_sem=hs.at[n - 1],
            recv_sem=hr.at[n - 1], device_id=device, device_id_type=MESH,
        )
        copy.start()
        copies.append(copy)

    def sent(r, carry):
        await_all(xbuf.at[r, pl.ds(0, 15)], xs.at[0])
        await_all(gsend.at[r, pl.ds(0, 15)], gs.at[0])
        for k in range(2):
            half_copy(r, k).wait_send()
        for k in range(4):
            core_copy(r, k).wait_send()
        for k in range(3):
            along_copy(r, k).wait_send()
        return carry

    lax.fori_loop(0, ROUNDS, sent, 0)
    for copy in copies:
        copy.wait()
    for r in range(ROUNDS):
        out[r * 2 : r * 2 + 2, :] = hsend[0, r] + (hrecv[0, r] + hrecv[1, r])


def local(spectra, dispersion, window_start, window_width, pupil):
    vmem = pltpu.VMEM
    dma = pltpu.SemaphoreType.DMA
    hbm = pl.BlockSpec(memory_space=pl.ANY)
    smem = pl.BlockSpec(memory_space=pltpu.SMEM)
    focused = pl.pallas_call(
        kernel,
        out_shape=jax.ShapeDtypeStruct((16, 256), F32),
        in_specs=[hbm, pl.BlockSpec(memory_space=pltpu.VMEM), smem, smem, hbm],
        out_specs=pl.BlockSpec(memory_space=pltpu.VMEM),
        scratch_shapes=[
            vmem((8, 2, 2, 64, 512), F32),
            vmem((8, 16, 64, 128), F32),
            vmem((8, 16, 64, 128), F32),
            vmem((K // 2, 256), BF16),
            vmem((512, K // 2), BF16),
            vmem((512, K // 2), BF16),
            vmem((32, K // 2), F32),
            vmem((32, K // 2), F32),
            vmem((8, K // 2), F32),
            vmem((8, K // 2), F32),
            vmem((2, 512, 512), F32),
            vmem((2, 2048, 512), BF16),
            vmem((2, 2048, 512), BF16),
            vmem((8, 4, 64, 128), F32),
            vmem((8, 2, 64, 128), F32),
            vmem((8, 16, 8, 128), F32),
            vmem((8, 16, 8, 128), F32),
            vmem((32, 1024), F32),
            vmem((8, 4, 32, 256), F32),
            vmem((8, 4, 32, 256), F32),
            vmem((8, 4, 32, 256), F32),
            vmem((8, 3, 32, 256), F32),
            vmem((3, 8, 2, 256), F32),
            vmem((2, 8, 2, 256), F32),
            dma((8,)), dma((1,)), dma((8,)), dma((8, 2)), dma((8, 2)), dma((1,)), dma((8,)),
            dma((8, 4)), dma((8, 4)), dma((8, 3)), dma((8, 3)), dma((2,)), dma((2,)), dma((2,)),
        ],
        compiler_params=pltpu.CompilerParams(
            collective_id=0, has_side_effects=True, vmem_limit_bytes=56 * 2**20
        ),
    )(
        jnp.swapaxes(spectra, 2, 3),
        dispersion.reshape(1, K),
        window_start,
        window_width,
        pupil,
    )
    return focused[None]


def solution(mesh):
    in_specs = (P(None, None, "pix", "spec"), P(), P(), P(), P(None, None, "pix"))
    out_specs = P("spec", None, "pix")
    return jax.shard_map(local, mesh=mesh, in_specs=in_specs, out_specs=out_specs, check_vma=False)
```

```python
import math

import jax
import jax.numpy as jnp
from jax import lax
from jax.experimental import pallas as pl
from jax.experimental.pallas import tpu as pltpu
from jax.sharding import PartitionSpec as P

K = 2048
MESH = pl.DeviceIdType.MESH
F32 = jnp.float32
BF16 = jnp.bfloat16
ROUNDS = 8
STEP = 2.0 * math.pi / K
LAST = ROUNDS - 1
SPLIT = 16


def split(values):
    high = values.astype(BF16)
    return high, (values - high.astype(F32)).astype(BF16)


def kernel(
    spectra, disp, start, width, pupil, out,
    staged, packed, xbuf, xhl, th, tl, cosa, sina, cosb, sinb, pstage, ph, plo,
    part, zrecv, gsend, grecv, glast, abuf, csend, own, crecv, frecv, hsend, hrecv,
    ls, xs, xr, zs, zr, gs, gr, cs, cr, fs, fr, hs, hr, ps, lsend, lr,
):
    s = lax.axis_index("spec")
    p = lax.axis_index("pix")
    me = s // 2
    zh = s % 2
    y = me // 4
    x = me % 4
    zl = p // 2
    co = p % 2
    partner = {"spec": s + 1 - 2 * zh}
    sibling = {"pix": zl * 2 + 1 - co}
    before = {"spec": (s + 31) % 32}
    after = {"spec": (s + 1) % 32}

    def peer(t):
        return ((y + t // 4) % 4) * 4 + (x + t % 4) % 4

    def along(dz):
        return (zl + dz) % 4

    barrier = pltpu.get_barrier_semaphore()

    def greet(t, carry):
        pl.semaphore_signal(
            barrier, inc=1, device_id={"spec": peer(t) * 2 + zh}, device_id_type=MESH
        )
        return carry

    lax.fori_loop(1, 16, greet, 0)
    for device in (partner, sibling, before, after):
        pl.semaphore_signal(barrier, inc=1, device_id=device, device_id_type=MESH)
    for dz in (1, 2, 3):
        pl.semaphore_signal(
            barrier, inc=1, device_id={"pix": along(dz) * 2 + co}, device_id_type=MESH
        )
    left = lax.broadcasted_iota(jnp.int32, (64, 128), 1) < 64
    left8 = lax.broadcasted_iota(jnp.int32, (8, 128), 1) < 64

    def load(r):
        return pltpu.make_async_copy(spectra.at[:, pl.ds(r * 2, 2)], staged.at[r], ls.at[r])

    def pack(r):
        load(r).wait()
        for i in range(2):
            for m in range(4):
                at = slice(m * 128, m * 128 + 128)
                real = staged[r, 0, i, :, at]
                imag = staged[r, 1, i, :, at]
                packed[r, i * 8 + m * 2] = jnp.where(left, real, pltpu.roll(imag, 64, 1))
                packed[r, i * 8 + m * 2 + 1] = jnp.where(left, pltpu.roll(real, 64, 1), imag)

    def send_blocks(r, first, last):
        def send(t, carry):
            j = peer(t)
            pltpu.make_async_remote_copy(
                src_ref=packed.at[r, j], dst_ref=xbuf.at[r, me], send_sem=xs.at[0],
                recv_sem=xr.at[r], device_id={"spec": j * 2 + zh}, device_id_type=MESH,
            ).start()
            return carry

        lax.fori_loop(first, last, send, 0)

    def keep_block(r):
        pltpu.make_async_copy(packed.at[r, me], xbuf.at[r, me], xr.at[r]).start()

    for r in range(ROUNDS):
        load(r).start()
    pack(0)
    pl.semaphore_wait(barrier, 22)
    send_blocks(0, 1, 16)
    keep_block(0)
    pack(1)
    send_blocks(1, 1, SPLIT)
    keep_block(1)

    def fetch(n, slot):
        return pltpu.make_async_copy(
            pupil.at[n // 4, pl.ds((n % 4) * 512, 512)], pstage.at[slot], ps.at[slot]
        )

    fetch(0, 0).start()

    HALF = K // 2
    lane = lax.broadcasted_iota(jnp.int32, (8, HALF), 1)
    wave = (lane // 64) * 128 + zh * 64 + lane % 64
    pieces = []
    for m in range(8):
        a = jnp.broadcast_to(disp[:, m * 256 : m * 256 + 128], (8, 128))
        b = jnp.broadcast_to(disp[:, m * 256 + 128 : m * 256 + 256], (8, 128))
        lower = jnp.where(left8, a, pltpu.roll(b, 64, 1))
        upper = jnp.where(left8, pltpu.roll(a, 64, 1), b)
        pieces.append(jnp.where(zh == 0, lower, upper))
    phase = jnp.concatenate(pieces, axis=1)
    fine = lax.broadcasted_iota(jnp.int32, (8, HALF), 0)
    beta = STEP * ((fine * wave) & (K - 1)).astype(F32) + phase
    scale = 1.0 / math.sqrt(K)
    cosb[...] = jnp.cos(beta) * scale
    sinb[...] = jnp.sin(beta) * scale

    def coarse(n, carry):
        row = lax.broadcasted_iota(jnp.int32, (8, HALF), 0) + n * 8
        zg = jnp.where(row < 16, 1 - zh, zh)
        q = (row % 16) * 2 + zg
        alpha = STEP * ((8 * q * wave) & (K - 1)).astype(F32)
        cosa[pl.ds(pl.multiple_of(n * 8, 8), 8), :] = jnp.cos(alpha)
        sina[pl.ds(pl.multiple_of(n * 8, 8), 8), :] = jnp.sin(alpha)
        return carry

    lax.fori_loop(0, 4, coarse, 0)

    def rows(n, carry):
        ca = cosa[pl.ds(n, 1), :]
        sa = sina[pl.ds(n, 1), :]
        real = ca * cosb[...] - sa * sinb[...]
        imag = -(sa * cosb[...] + ca * sinb[...])
        high, low = split(jnp.concatenate([real, imag], axis=0))
        at = pl.ds(pl.multiple_of(n * 16, 16), 16)
        th[at, :] = high
        tl[at, :] = low
        return carry

    lax.fori_loop(0, 32, rows, 0)

    def convert(n, carry):
        slot = n % 2

        @pl.when(n < 7)
        def _():
            fetch(n + 1, 1 - slot).start()

        fetch(n, slot).wait()

        def piece(m, inner):
            rows_at = pl.ds(pl.multiple_of(m * 128, 128), 128)
            high, low = split(pstage[slot, rows_at, :].T)
            at = pl.ds(pl.multiple_of((n % 4) * 512 + m * 128, 128), 128)
            ph[n // 4, :, at] = high
            plo[n // 4, :, at] = low
            return inner

        lax.fori_loop(0, 4, piece, 0)
        return carry

    def convert_some(first, last):
        lax.fori_loop(first, last, convert, 0)

    convert_some(0, 3)

    def await_all(ref, sem):
        pltpu.make_async_copy(ref, ref, sem).wait()

    def half_copy(r, k):
        return pltpu.make_async_remote_copy(
            src_ref=part.at[r, k], dst_ref=zrecv.at[r, k], send_sem=zs.at[r, k],
            recv_sem=zr.at[r, k], device_id=partner, device_id_type=MESH,
        )

    def core_copy(r, k):
        return pltpu.make_async_remote_copy(
            src_ref=csend.at[r, k], dst_ref=crecv.at[r, k], send_sem=cs.at[r, k],
            recv_sem=cr.at[r, k], device_id=sibling, device_id_type=MESH,
        )

    def along_copy(r, k):
        return pltpu.make_async_remote_copy(
            src_ref=own.at[r, k], dst_ref=frecv.at[r, k], send_sem=fs.at[r, k],
            recv_sem=fr.at[r, k], device_id={"pix": along(k + 1) * 2 + co}, device_id_type=MESH,
        )

    def gates(half, j):
        at = pl.ds(pl.multiple_of((j % 8) * 8, 8), 8)
        return part.at[LAST, half * 2 + j // 8, at]

    def across(t, carry):
        j = peer(t)
        pltpu.make_async_remote_copy(
            src_ref=gates(0, j), dst_ref=glast.at[0, me], send_sem=lsend.at[0],
            recv_sem=lr.at[0], device_id={"spec": j * 2 + 1 - zh}, device_id_type=MESH,
        ).start()
        return carry

    def within(t, carry):
        j = peer(t)
        pltpu.make_async_remote_copy(
            src_ref=gates(1, j), dst_ref=glast.at[1, me], send_sem=lsend.at[1],
            recv_sem=lr.at[1], device_id={"spec": j * 2 + zh}, device_id_type=MESH,
        ).start()
        return carry

    def transform(r):
        await_all(xbuf.at[r], xr.at[r])

        def piece(n, carry):
            high, low = split(xbuf[r, pl.ds(n * 2, 2)].reshape(128, 128))
            at = pl.ds(pl.multiple_of(n * 128, 128), 128)
            xhl[at, 0:128] = high
            xhl[at, 128:256] = low
            return carry

        lax.fori_loop(0, 8, piece, 0)
        for half in (0, 1):
            at = slice(half * 256, half * 256 + 256)
            both = jnp.dot(th[at, :], xhl[...], preferred_element_type=F32)
            rest = jnp.dot(tl[at, :], xhl[:, 0:128], preferred_element_type=F32)
            done = (both[:, 0:128] + (both[:, 128:256] + rest)).reshape(16, 2, 8, 128)
            straight = done[:, 0].reshape(128, 128)
            crossed = pltpu.roll(done[:, 1].reshape(128, 128), 64, 1)
            left128 = lax.broadcasted_iota(jnp.int32, (128, 128), 1) < 64
            field = straight + jnp.where(left128, -crossed, crossed)
            part[r, half * 2] = field[0:64]
            part[r, half * 2 + 1] = field[64:128]
            if half == 0:
                @pl.when(r < LAST)
                def _():
                    half_copy(r, 0).start()
                    half_copy(r, 1).start()

                @pl.when(r == LAST)
                def _():
                    lax.fori_loop(0, 16, across, 0)

            else:
                @pl.when(r == LAST)
                def _():
                    lax.fori_loop(1, 16, within, 0)
                    pltpu.make_async_copy(gates(1, me), glast.at[1, me], lr.at[1]).start()

    def hand_out(r):
        def send(j):
            @pl.when(j != me)
            def _():
                pltpu.make_async_remote_copy(
                    src_ref=gsend.at[r, j], dst_ref=grecv.at[r, me], send_sem=gs.at[0],
                    recv_sem=gr.at[r], device_id={"spec": j * 2 + zh}, device_id_type=MESH,
                ).start()

        def ordered(t, carry):
            send(carry + ((t + me) % 8))
            return carry

        for k in (0, 1):
            half_copy(r, k).wait_recv()
            gsend[r, pl.ds(k * 8, 8)] = (part[r, 2 + k] + zrecv[r, k]).reshape(8, 8, 128)
            lax.fori_loop(0, 8, ordered, k * 8)
        pltpu.make_async_copy(gsend.at[r, me], grecv.at[r, me], gr.at[r]).start()

    def collect(r, q):
        for i in range(2):
            for m in range(4):
                a = grecv[r, i * 8 + m * 2]
                b = grecv[r, i * 8 + m * 2 + 1]
                real = jnp.where(left8, a, pltpu.roll(b, 64, 1))
                imag = jnp.where(left8, pltpu.roll(a, 64, 1), b)
                row = q * 32 + i * 8
                col = m * 128
                abuf[row : row + 8, col : col + 128] = real
                abuf[row : row + 8, 512 + col : 640 + col] = -imag
                abuf[16 + row : 24 + row, col : col + 128] = imag
                abuf[16 + row : 24 + row, 512 + col : 640 + col] = real

    def project(r, count):
        for q in range(count):
            collect(r + q, q)
        size = count * 32
        high, low = split(abuf[0:size, :])
        stack = jnp.concatenate([high, low], axis=0)

        def product(b, core):
            at = pl.ds(pl.multiple_of((b * 2 + core) * 256, 256), 256)
            both = jnp.dot(stack[:, 0:512], ph[0, :, at], preferred_element_type=F32) + jnp.dot(
                stack[:, 512:1024], ph[1, :, at], preferred_element_type=F32
            )
            rest = jnp.dot(high[:, 0:512], plo[0, :, at], preferred_element_type=F32) + jnp.dot(
                high[:, 512:1024], plo[1, :, at], preferred_element_type=F32
            )
            return both[0:size] + (both[size : 2 * size] + rest)

        def give(k):
            values = product(along(k + 1), 1 - co)
            for q in range(count):
                csend[r + q, k] = values[q * 32 : q * 32 + 32]
                core_copy(r + q, k).start()

        def first(k, carry):
            give(k)
            return carry

        lax.fori_loop(0, 4, first, 0)

        def step(k, carry):
            mine = product(along(k + 1), co)
            for q in range(count):
                core_copy(r + q, k).wait_recv()
                own[r + q, k] = mine[q * 32 : q * 32 + 32] + crecv[r + q, k]

            @pl.when(k < 3)
            def _():
                for q in range(count):
                    along_copy(r + q, k).start()

            return carry

        lax.fori_loop(0, 4, step, 0)

    def project_one(r):
        @pl.when(r < LAST)
        def _():
            await_all(grecv.at[r], gr.at[r])

        @pl.when(r == LAST)
        def _():
            await_all(glast.at[0], lr.at[0])
            await_all(glast.at[1], lr.at[1])
            grecv[r] = glast[0] + glast[1]

        project(r, 1)

    def project_two(r):
        for q in range(2):
            await_all(grecv.at[r + q], gr.at[r + q])
        project(r, 2)

    gate = s * 8 + lax.broadcasted_iota(jnp.int32, (8, 256), 0)

    def weight(owner):
        first = start[owner]
        return ((gate >= first) & (gate < first + width[owner])).astype(F32)

    def finish(r):
        for k in range(3):
            along_copy(r, k).wait_recv()
        total = own[r, 3] + (frecv[r, 0] + (frecv[r, 1] + frecv[r, 2]))
        power = total[0:16] * total[0:16] + total[16:32] * total[16:32]
        for n, owner in enumerate((s, (s + 31) % 32, (s + 1) % 32)):
            w = weight(owner)
            for i in range(2):
                hsend[n, r, i : i + 1, :] = jnp.sum(
                    power[i * 8 : i * 8 + 8] * w, axis=0, keepdims=True
                )

    def turn(n, carry):
        pl.when(n < 8)(lambda: transform(n))
        pl.when((n >= 1) & (n < 8))(lambda: hand_out(n - 1))
        pl.when(n < 7)(lambda: send_blocks(n + 1, SPLIT, 16))

        @pl.when(n < 6)
        def _():
            pack(n + 2)
            send_blocks(n + 2, 1, SPLIT)
            keep_block(n + 2)

        pl.when(n == 0)(lambda: convert_some(3, 6))
        pl.when(n == 1)(lambda: convert_some(6, 8))
        pl.when(n >= 2)(lambda: project_one(n - 2))
        pl.when((n >= 3) & (n < 9))(lambda: finish(n - 3))
        return carry

    lax.fori_loop(0, ROUNDS + 2, turn, 0)
    finish(6)
    finish(7)

    copies = []
    for n, device in ((1, before), (2, after)):
        copy = pltpu.make_async_remote_copy(
            src_ref=hsend.at[n], dst_ref=hrecv.at[n - 1], send_sem=hs.at[n - 1],
            recv_sem=hr.at[n - 1], device_id=device, device_id_type=MESH,
        )
        copy.start()
        copies.append(copy)

    def sent(r, carry):
        await_all(xbuf.at[r, pl.ds(0, 15)], xs.at[0])

        @pl.when(r < LAST)
        def _():
            await_all(gsend.at[r, pl.ds(0, 15)], gs.at[0])
            for k in range(2):
                half_copy(r, k).wait_send()

        for k in range(4):
            core_copy(r, k).wait_send()
        for k in range(3):
            along_copy(r, k).wait_send()
        return carry

    lax.fori_loop(0, ROUNDS, sent, 0)
    await_all(glast.at[0], lsend.at[0])
    await_all(glast.at[1, pl.ds(0, 15)], lsend.at[1])
    for copy in copies:
        copy.wait()
    for r in range(ROUNDS):
        out[r * 2 : r * 2 + 2, :] = hsend[0, r] + (hrecv[0, r] + hrecv[1, r])


def local(spectra, dispersion, window_start, window_width, pupil):
    vmem = pltpu.VMEM
    dma = pltpu.SemaphoreType.DMA
    hbm = pl.BlockSpec(memory_space=pl.ANY)
    smem = pl.BlockSpec(memory_space=pltpu.SMEM)
    focused = pl.pallas_call(
        kernel,
        out_shape=jax.ShapeDtypeStruct((16, 256), F32),
        in_specs=[hbm, pl.BlockSpec(memory_space=pltpu.VMEM), smem, smem, hbm],
        out_specs=pl.BlockSpec(memory_space=pltpu.VMEM),
        scratch_shapes=[
            vmem((8, 2, 2, 64, 512), F32),
            vmem((8, 16, 64, 128), F32),
            vmem((8, 16, 64, 128), F32),
            vmem((K // 2, 256), BF16),
            vmem((512, K // 2), BF16),
            vmem((512, K // 2), BF16),
            vmem((32, K // 2), F32),
            vmem((32, K // 2), F32),
            vmem((8, K // 2), F32),
            vmem((8, K // 2), F32),
            vmem((2, 512, 512), F32),
            vmem((2, 512, 2048), BF16),
            vmem((2, 512, 2048), BF16),
            vmem((8, 4, 64, 128), F32),
            vmem((8, 2, 64, 128), F32),
            vmem((8, 16, 8, 128), F32),
            vmem((8, 16, 8, 128), F32),
            vmem((2, 16, 8, 128), F32),
            vmem((64, 1024), F32),
            vmem((8, 4, 32, 256), F32),
            vmem((8, 4, 32, 256), F32),
            vmem((8, 4, 32, 256), F32),
            vmem((8, 3, 32, 256), F32),
            vmem((3, 8, 2, 256), F32),
            vmem((2, 8, 2, 256), F32),
            dma((8,)), dma((1,)), dma((8,)), dma((8, 2)), dma((8, 2)), dma((1,)), dma((8,)),
            dma((8, 4)), dma((8, 4)), dma((8, 3)), dma((8, 3)), dma((2,)), dma((2,)), dma((2,)), dma((2,)), dma((2,)),
        ],
        compiler_params=pltpu.CompilerParams(
            collective_id=0, has_side_effects=True, vmem_limit_bytes=56 * 2**20
        ),
    )(
        jnp.swapaxes(spectra, 2, 3),
        dispersion.reshape(1, K),
        window_start,
        window_width,
        pupil,
    )
    return focused[None]


def solution(mesh):
    in_specs = (P(None, None, "pix", "spec"), P(), P(), P(), P(None, None, "pix"))
    out_specs = P("spec", None, "pix")
    return jax.shard_map(local, mesh=mesh, in_specs=in_specs, out_specs=out_specs, check_vma=False)
```

```python
import math

import jax
import jax.numpy as jnp
from jax import lax
from jax.experimental import pallas as pl
from jax.experimental.pallas import tpu as pltpu
from jax.sharding import PartitionSpec as P

K = 2048
MESH = pl.DeviceIdType.MESH
F32 = jnp.float32
BF16 = jnp.bfloat16
ROUNDS = 8
STEP = 2.0 * math.pi / K
LAST = ROUNDS - 1


def hops(t):
    return min(t % 4, 4 - t % 4) + min(t // 4, 4 - t // 4)


NEAR = sorted(range(1, 16), key=hops)


def split(values):
    high = values.astype(BF16)
    return high, (values - high.astype(F32)).astype(BF16)


def kernel(
    spectra, disp, start, width, pupil, out,
    staged, packed, xbuf, xhl, th, tl, cosa, sina, cosb, sinb, pstage, ph, plo,
    part, zrecv, gsend, grecv, glast, abuf, csend, own, crecv, frecv, hsend, hrecv,
    ls, xs, xr, zs, zr, gs, gr, cs, cr, fs, fr, hs, hr, ps, lsend, lr,
):
    s = lax.axis_index("spec")
    p = lax.axis_index("pix")
    me = s // 2
    zh = s % 2
    y = me // 4
    x = me % 4
    zl = p // 2
    co = p % 2
    partner = {"spec": s + 1 - 2 * zh}
    sibling = {"pix": zl * 2 + 1 - co}
    before = {"spec": (s + 31) % 32}
    after = {"spec": (s + 1) % 32}

    def peer(t):
        return ((y + t // 4) % 4) * 4 + (x + t % 4) % 4

    def along(dz):
        return (zl + dz) % 4

    barrier = pltpu.get_barrier_semaphore()

    def greet(t, carry):
        pl.semaphore_signal(
            barrier, inc=1, device_id={"spec": peer(t) * 2 + zh}, device_id_type=MESH
        )
        return carry

    lax.fori_loop(1, 16, greet, 0)
    for device in (partner, sibling, before, after):
        pl.semaphore_signal(barrier, inc=1, device_id=device, device_id_type=MESH)
    for dz in (1, 2, 3):
        pl.semaphore_signal(
            barrier, inc=1, device_id={"pix": along(dz) * 2 + co}, device_id_type=MESH
        )
    left = lax.broadcasted_iota(jnp.int32, (64, 128), 1) < 64
    left8 = lax.broadcasted_iota(jnp.int32, (8, 128), 1) < 64

    def load(r):
        return pltpu.make_async_copy(spectra.at[:, pl.ds(r * 2, 2)], staged.at[r], ls.at[r])

    def pack(r):
        load(r).wait()
        for i in range(2):
            for m in range(4):
                at = slice(m * 128, m * 128 + 128)
                real = staged[r, 0, i, :, at]
                imag = staged[r, 1, i, :, at]
                packed[r, i * 8 + m * 2] = jnp.where(left, real, pltpu.roll(imag, 64, 1))
                packed[r, i * 8 + m * 2 + 1] = jnp.where(left, pltpu.roll(real, 64, 1), imag)

    def send_blocks(r):
        for t in NEAR:
            j = peer(t)
            pltpu.make_async_remote_copy(
                src_ref=packed.at[r, j], dst_ref=xbuf.at[r, me], send_sem=xs.at[0],
                recv_sem=xr.at[r], device_id={"spec": j * 2 + zh}, device_id_type=MESH,
            ).start()

    def keep_block(r):
        pltpu.make_async_copy(packed.at[r, me], xbuf.at[r, me], xr.at[r]).start()

    for r in range(ROUNDS):
        load(r).start()
    pack(0)
    pl.semaphore_wait(barrier, 22)
    send_blocks(0)
    keep_block(0)
    pack(1)
    send_blocks(1)
    keep_block(1)

    def fetch(n, slot):
        return pltpu.make_async_copy(
            pupil.at[n // 4, pl.ds((n % 4) * 512, 512)], pstage.at[slot], ps.at[slot]
        )

    fetch(0, 0).start()

    HALF = K // 2
    lane = lax.broadcasted_iota(jnp.int32, (8, HALF), 1)
    wave = (lane // 64) * 128 + zh * 64 + lane % 64
    pieces = []
    for m in range(8):
        a = jnp.broadcast_to(disp[:, m * 256 : m * 256 + 128], (8, 128))
        b = jnp.broadcast_to(disp[:, m * 256 + 128 : m * 256 + 256], (8, 128))
        lower = jnp.where(left8, a, pltpu.roll(b, 64, 1))
        upper = jnp.where(left8, pltpu.roll(a, 64, 1), b)
        pieces.append(jnp.where(zh == 0, lower, upper))
    phase = jnp.concatenate(pieces, axis=1)
    fine = lax.broadcasted_iota(jnp.int32, (8, HALF), 0)
    beta = STEP * ((fine * wave) & (K - 1)).astype(F32) + phase
    scale = 1.0 / math.sqrt(K)
    cosb[...] = jnp.cos(beta) * scale
    sinb[...] = jnp.sin(beta) * scale

    def coarse(n, carry):
        row = lax.broadcasted_iota(jnp.int32, (8, HALF), 0) + n * 8
        zg = jnp.where(row < 16, 1 - zh, zh)
        q = (row % 16) * 2 + zg
        alpha = STEP * ((8 * q * wave) & (K - 1)).astype(F32)
        cosa[pl.ds(pl.multiple_of(n * 8, 8), 8), :] = jnp.cos(alpha)
        sina[pl.ds(pl.multiple_of(n * 8, 8), 8), :] = jnp.sin(alpha)
        return carry

    lax.fori_loop(0, 4, coarse, 0)

    def rows(n, carry):
        ca = cosa[pl.ds(n, 1), :]
        sa = sina[pl.ds(n, 1), :]
        real = ca * cosb[...] - sa * sinb[...]
        imag = -(sa * cosb[...] + ca * sinb[...])
        high, low = split(jnp.concatenate([real, imag], axis=0))
        at = pl.ds(pl.multiple_of(n * 16, 16), 16)
        th[at, :] = high
        tl[at, :] = low
        return carry

    lax.fori_loop(0, 32, rows, 0)

    def convert(n, carry):
        slot = n % 2

        @pl.when(n < 7)
        def _():
            fetch(n + 1, 1 - slot).start()

        fetch(n, slot).wait()

        def piece(m, inner):
            rows_at = pl.ds(pl.multiple_of(m * 128, 128), 128)
            high, low = split(pstage[slot, rows_at, :].T)
            at = pl.ds(pl.multiple_of((n % 4) * 512 + m * 128, 128), 128)
            ph[n // 4, :, at] = high
            plo[n // 4, :, at] = low
            return inner

        lax.fori_loop(0, 4, piece, 0)
        return carry

    def convert_some(first, last):
        lax.fori_loop(first, last, convert, 0)

    convert_some(0, 3)

    def await_all(ref, sem):
        pltpu.make_async_copy(ref, ref, sem).wait()

    def half_copy(r):
        return pltpu.make_async_remote_copy(
            src_ref=part.at[r, pl.ds(0, 2)], dst_ref=zrecv.at[r], send_sem=zs.at[r],
            recv_sem=zr.at[r], device_id=partner, device_id_type=MESH,
        )

    def core_copy(r, k):
        return pltpu.make_async_remote_copy(
            src_ref=csend.at[r, k], dst_ref=crecv.at[r, k], send_sem=cs.at[r, k],
            recv_sem=cr.at[r, k], device_id=sibling, device_id_type=MESH,
        )

    def along_copy(r, k):
        return pltpu.make_async_remote_copy(
            src_ref=own.at[r, k], dst_ref=frecv.at[r, k], send_sem=fs.at[r, k],
            recv_sem=fr.at[r, k], device_id={"pix": along(k + 1) * 2 + co}, device_id_type=MESH,
        )

    def gates(half, j):
        at = pl.ds(pl.multiple_of((j % 8) * 8, 8), 8)
        return part.at[LAST, half * 2 + j // 8, at]

    def across(t, carry):
        j = peer(t)
        pltpu.make_async_remote_copy(
            src_ref=gates(0, j), dst_ref=glast.at[0, me], send_sem=lsend.at[0],
            recv_sem=lr.at[0], device_id={"spec": j * 2 + 1 - zh}, device_id_type=MESH,
        ).start()
        return carry

    def within(t, carry):
        j = peer(t)
        pltpu.make_async_remote_copy(
            src_ref=gates(1, j), dst_ref=glast.at[1, me], send_sem=lsend.at[1],
            recv_sem=lr.at[1], device_id={"spec": j * 2 + zh}, device_id_type=MESH,
        ).start()
        return carry

    def transform(r):
        await_all(xbuf.at[r], xr.at[r])

        def piece(n, carry):
            high, low = split(xbuf[r, pl.ds(n * 2, 2)].reshape(128, 128))
            at = pl.ds(pl.multiple_of(n * 128, 128), 128)
            xhl[at, 0:128] = high
            xhl[at, 128:256] = low
            return carry

        lax.fori_loop(0, 8, piece, 0)
        for half in (0, 1):
            at = slice(half * 256, half * 256 + 256)
            both = jnp.dot(th[at, :], xhl[...], preferred_element_type=F32)
            rest = jnp.dot(tl[at, :], xhl[:, 0:128], preferred_element_type=F32)
            done = (both[:, 0:128] + (both[:, 128:256] + rest)).reshape(16, 2, 8, 128)
            straight = done[:, 0].reshape(128, 128)
            crossed = pltpu.roll(done[:, 1].reshape(128, 128), 64, 1)
            left128 = lax.broadcasted_iota(jnp.int32, (128, 128), 1) < 64
            field = straight + jnp.where(left128, -crossed, crossed)
            part[r, half * 2] = field[0:64]
            part[r, half * 2 + 1] = field[64:128]
            if half == 0:
                @pl.when(r < LAST)
                def _():
                    half_copy(r).start()

                @pl.when(r == LAST)
                def _():
                    lax.fori_loop(0, 16, across, 0)

            else:
                @pl.when(r == LAST)
                def _():
                    lax.fori_loop(1, 16, within, 0)
                    pltpu.make_async_copy(gates(1, me), glast.at[1, me], lr.at[1]).start()

    def hand_out(r):
        half_copy(r).wait_recv()
        gsend[r] = (part[r, 2:4] + zrecv[r]).reshape(16, 8, 128)
        for t in NEAR:
            j = peer(t)
            pltpu.make_async_remote_copy(
                src_ref=gsend.at[r, j], dst_ref=grecv.at[r, me], send_sem=gs.at[0],
                recv_sem=gr.at[r], device_id={"spec": j * 2 + zh}, device_id_type=MESH,
            ).start()
        pltpu.make_async_copy(gsend.at[r, me], grecv.at[r, me], gr.at[r]).start()

    def collect(r, q):
        for i in range(2):
            for m in range(4):
                a = grecv[r, i * 8 + m * 2]
                b = grecv[r, i * 8 + m * 2 + 1]
                real = jnp.where(left8, a, pltpu.roll(b, 64, 1))
                imag = jnp.where(left8, pltpu.roll(a, 64, 1), b)
                row = q * 32 + i * 8
                col = m * 128
                abuf[row : row + 8, col : col + 128] = real
                abuf[row : row + 8, 512 + col : 640 + col] = -imag
                abuf[16 + row : 24 + row, col : col + 128] = imag
                abuf[16 + row : 24 + row, 512 + col : 640 + col] = real

    def project(r, count):
        for q in range(count):
            collect(r + q, q)
        size = count * 32
        high, low = split(abuf[0:size, :])
        stack = jnp.concatenate([high, low], axis=0)

        def product(b, core):
            at = pl.ds(pl.multiple_of((b * 2 + core) * 256, 256), 256)
            both = jnp.dot(stack[:, 0:512], ph[0, :, at], preferred_element_type=F32) + jnp.dot(
                stack[:, 512:1024], ph[1, :, at], preferred_element_type=F32
            )
            rest = jnp.dot(high[:, 0:512], plo[0, :, at], preferred_element_type=F32) + jnp.dot(
                high[:, 512:1024], plo[1, :, at], preferred_element_type=F32
            )
            return both[0:size] + (both[size : 2 * size] + rest)

        def give(k):
            values = product(along(k + 1), 1 - co)
            for q in range(count):
                csend[r + q, k] = values[q * 32 : q * 32 + 32]
                core_copy(r + q, k).start()

        def first(k, carry):
            give(k)
            return carry

        lax.fori_loop(0, 4, first, 0)

        def step(k, carry):
            mine = product(along(k + 1), co)
            for q in range(count):
                core_copy(r + q, k).wait_recv()
                own[r + q, k] = mine[q * 32 : q * 32 + 32] + crecv[r + q, k]

            @pl.when(k < 3)
            def _():
                for q in range(count):
                    along_copy(r + q, k).start()

            return carry

        lax.fori_loop(0, 4, step, 0)

    def project_one(r):
        @pl.when(r < LAST)
        def _():
            await_all(grecv.at[r], gr.at[r])

        @pl.when(r == LAST)
        def _():
            await_all(glast.at[0], lr.at[0])
            await_all(glast.at[1], lr.at[1])
            grecv[r] = glast[0] + glast[1]

        project(r, 1)

    def project_two(r):
        for q in range(2):
            await_all(grecv.at[r + q], gr.at[r + q])
        project(r, 2)

    gate = s * 8 + lax.broadcasted_iota(jnp.int32, (8, 256), 0)

    def weight(owner):
        first = start[owner]
        return ((gate >= first) & (gate < first + width[owner])).astype(F32)

    def finish(r):
        for k in range(3):
            along_copy(r, k).wait_recv()
        total = own[r, 3] + (frecv[r, 0] + (frecv[r, 1] + frecv[r, 2]))
        power = total[0:16] * total[0:16] + total[16:32] * total[16:32]
        for n, owner in enumerate((s, (s + 31) % 32, (s + 1) % 32)):
            w = weight(owner)
            for i in range(2):
                hsend[n, r, i : i + 1, :] = jnp.sum(
                    power[i * 8 : i * 8 + 8] * w, axis=0, keepdims=True
                )

    def turn(n, carry):
        pl.when(n < 8)(lambda: transform(n))
        pl.when((n >= 1) & (n < 8))(lambda: hand_out(n - 1))

        @pl.when(n < 6)
        def _():
            pack(n + 2)
            send_blocks(n + 2)
            keep_block(n + 2)

        pl.when(n == 0)(lambda: convert_some(3, 6))
        pl.when(n == 1)(lambda: convert_some(6, 8))
        pl.when(n >= 2)(lambda: project_one(n - 2))
        pl.when((n >= 3) & (n < 9))(lambda: finish(n - 3))
        return carry

    lax.fori_loop(0, ROUNDS + 2, turn, 0)
    finish(6)
    finish(7)

    copies = []
    for n, device in ((1, before), (2, after)):
        copy = pltpu.make_async_remote_copy(
            src_ref=hsend.at[n], dst_ref=hrecv.at[n - 1], send_sem=hs.at[n - 1],
            recv_sem=hr.at[n - 1], device_id=device, device_id_type=MESH,
        )
        copy.start()
        copies.append(copy)

    def sent(r, carry):
        await_all(xbuf.at[r, pl.ds(0, 15)], xs.at[0])

        @pl.when(r < LAST)
        def _():
            await_all(gsend.at[r, pl.ds(0, 15)], gs.at[0])
            half_copy(r).wait_send()

        for k in range(4):
            core_copy(r, k).wait_send()
        for k in range(3):
            along_copy(r, k).wait_send()
        return carry

    lax.fori_loop(0, ROUNDS, sent, 0)
    await_all(glast.at[0], lsend.at[0])
    await_all(glast.at[1, pl.ds(0, 15)], lsend.at[1])
    for copy in copies:
        copy.wait()
    for r in range(ROUNDS):
        out[r * 2 : r * 2 + 2, :] = hsend[0, r] + (hrecv[0, r] + hrecv[1, r])


def local(spectra, dispersion, window_start, window_width, pupil):
    vmem = pltpu.VMEM
    dma = pltpu.SemaphoreType.DMA
    hbm = pl.BlockSpec(memory_space=pl.ANY)
    smem = pl.BlockSpec(memory_space=pltpu.SMEM)
    focused = pl.pallas_call(
        kernel,
        out_shape=jax.ShapeDtypeStruct((16, 256), F32),
        in_specs=[hbm, pl.BlockSpec(memory_space=pltpu.VMEM), smem, smem, hbm],
        out_specs=pl.BlockSpec(memory_space=pltpu.VMEM),
        scratch_shapes=[
            vmem((8, 2, 2, 64, 512), F32),
            vmem((8, 16, 64, 128), F32),
            vmem((8, 16, 64, 128), F32),
            vmem((K // 2, 256), BF16),
            vmem((512, K // 2), BF16),
            vmem((512, K // 2), BF16),
            vmem((32, K // 2), F32),
            vmem((32, K // 2), F32),
            vmem((8, K // 2), F32),
            vmem((8, K // 2), F32),
            vmem((2, 512, 512), F32),
            vmem((2, 512, 2048), BF16),
            vmem((2, 512, 2048), BF16),
            vmem((8, 4, 64, 128), F32),
            vmem((8, 2, 64, 128), F32),
            vmem((8, 16, 8, 128), F32),
            vmem((8, 16, 8, 128), F32),
            vmem((2, 16, 8, 128), F32),
            vmem((64, 1024), F32),
            vmem((8, 4, 32, 256), F32),
            vmem((8, 4, 32, 256), F32),
            vmem((8, 4, 32, 256), F32),
            vmem((8, 3, 32, 256), F32),
            vmem((3, 8, 2, 256), F32),
            vmem((2, 8, 2, 256), F32),
            dma((8,)), dma((1,)), dma((8,)), dma((8,)), dma((8,)), dma((1,)), dma((8,)),
            dma((8, 4)), dma((8, 4)), dma((8, 3)), dma((8, 3)), dma((2,)), dma((2,)), dma((2,)), dma((2,)), dma((2,)),
        ],
        compiler_params=pltpu.CompilerParams(
            collective_id=0, has_side_effects=True, vmem_limit_bytes=56 * 2**20
        ),
    )(
        jnp.swapaxes(spectra, 2, 3),
        dispersion.reshape(1, K),
        window_start,
        window_width,
        pupil,
    )
    return focused[None]


def solution(mesh):
    in_specs = (P(None, None, "pix", "spec"), P(), P(), P(), P(None, None, "pix"))
    out_specs = P("spec", None, "pix")
    return jax.shard_map(local, mesh=mesh, in_specs=in_specs, out_specs=out_specs, check_vma=False)
```
